512 devices in a mesh: cmp: 32 (over z, x), tgt: 16 (over y, core).
Axes of the slice: x: 4, y: 8, z: 8, core: 2. Of those that a mesh axis runs over, the one named last changes fastest.
Arguments:
- responses: bfloat16 [8192, 1024, 128], P('cmp', 'tgt'), may hold values from -33 to 33
- target_init: bfloat16 [1024, 64], P('tgt'), may hold values from -5 to 5
- condition_factor: bfloat16 [128, 64], replicated, may hold values from -0.5 to 0.5
Outputs:
- compound_factor: float32 [8192, 64], P('cmp')
- target_factor: float32 [1024, 64], P('tgt')
The draws below stay inside these ranges and needn't reach their ends.
All inputs are finite; a program needn't handle non-finite values.
Results may differ from the reference program's by a relative error of at most 0.0003.
Values sent between devices are 32-bit elements; how exact they have to be, the bound alone decides.
A program may use at most 64 MiB of HBM per device.

```python
import jax
import jax.numpy as jnp
from jax import lax

CMP_DEV = 256
CONDITIONS = 128
RANK = 64
ITERS = 5
COMPOUNDS = 8192
TARGETS = 1024
N_CMP = 32


def draw_responses(key, part):
    key_rows, key_cols, key_conds, key_base = jax.random.split(key, 4)
    row_pos = jnp.arange(COMPOUNDS, dtype=jnp.float32) / max(COMPOUNDS - 1, 1)
    col_pos = jnp.arange(TARGETS, dtype=jnp.float32) / max(TARGETS - 1, 1)
    row_scale = jnp.exp(jnp.log(3.0) * row_pos + jnp.log(3.0) * jax.random.uniform(key_rows, (COMPOUNDS,)))
    col_scale = jnp.exp(jnp.log(3.0) * col_pos + jnp.log(3.0) * jax.random.uniform(key_cols, (TARGETS,)))
    cond_scale = jnp.exp(jnp.log(2.0) * jax.random.uniform(key_conds, (CONDITIONS,)))
    scale = row_scale[:, None, None] * col_scale[None, :, None] * cond_scale[None, None, :] / 20.0
    shape = (COMPOUNDS, TARGETS, CONDITIONS)
    base = jnp.clip(jax.random.normal(key_base, shape), -4.0, 4.0)
    return (base * scale).astype(jnp.bfloat16)


def block_scale(stream_key, dims, cuts, low, top_value):
    def one(dim, blocks):
        heights = jax.random.uniform(jax.random.fold_in(jax.random.fold_in(stream_key, 6), dim), (blocks,), jnp.float32, low / len(cuts), top_value / len(cuts))
        return jnp.repeat(jnp.exp(heights), dims[dim] // blocks).reshape((-1,) + (1,) * (len(dims) - dim - 1))

    gain = one(*cuts[0])
    for cut in cuts[1:]:
        gain = gain * one(*cut)
    return gain


def scatter_about(key, extent, width, most, cuts=(), held_as=jnp.bfloat16):
    factor_of = block_scale(key, extent, cuts, -0.22, 0.18) if cuts else 1.0
    entries = jax.random.normal(key, extent, jnp.float32) * width * factor_of
    return jnp.minimum(jnp.maximum(entries, -most), most).astype(held_as)


def setup_inputs(seed: int = 0) -> dict:
    keys = jax.random.split(jax.random.key(seed), 4)
    responses = draw_responses(jax.random.fold_in(keys[3], 71), 0)
    target_init = scatter_about(keys[1], (TARGETS, RANK), 1.0, 5.0, ((0, 16),))
    condition_factor = scatter_about(keys[2], (CONDITIONS, RANK), CONDITIONS ** -0.5, 0.5)
    return dict(responses=responses, target_init=target_init, condition_factor=condition_factor)


def gram_of(factor):
    return jnp.dot(factor.T.astype(jnp.float32), factor.astype(jnp.float32), precision=lax.Precision.HIGHEST, preferred_element_type=jnp.float32)

def solve_normal(rhs, normal):
    lower = jnp.linalg.cholesky(normal)
    middle = lax.linalg.triangular_solve(lower, rhs, left_side=False, lower=True, transpose_a=True)
    return lax.linalg.triangular_solve(lower, middle, left_side=False, lower=True, transpose_a=False)

def reference(responses, target_init, condition_factor):
    cond = condition_factor.astype(jnp.float32)
    blocks = responses.reshape(N_CMP, CMP_DEV, TARGETS, CONDITIONS)

    def contract(block):
        return jnp.einsum('ijk,kr->ijr', block.astype(jnp.float32), cond, precision=lax.Precision.HIGHEST)
    inner = lax.map(contract, blocks).reshape(COMPOUNDS, TARGETS, RANK)
    cond_gram = gram_of(cond)
    target_raw = target_init.astype(jnp.float32)
    target_gram = gram_of(target_raw)
    compound_raw = jnp.zeros((COMPOUNDS, RANK), jnp.float32)
    compound_gram = jnp.zeros((RANK, RANK), jnp.float32)
    for sweep in range(ITERS):
        first = jnp.einsum('ijr,jr->ir', inner, target_raw, precision=lax.Precision.HIGHEST)
        compound_raw = solve_normal(first, target_gram * cond_gram)
        compound_gram = gram_of(compound_raw)
        second = jnp.einsum('ijr,ir->jr', inner, compound_raw, precision=lax.Precision.HIGHEST)
        target_raw = solve_normal(second, compound_gram * cond_gram)
        target_gram = gram_of(target_raw)
    compound_factor = compound_raw / jnp.sqrt(jnp.diagonal(compound_gram) / COMPOUNDS + 1e-06)[None, :]
    target_factor = target_raw / jnp.sqrt(jnp.diagonal(target_gram) / TARGETS + 1e-06)[None, :]
    return (compound_factor, target_factor)
```

```python
import functools

import jax
import jax.numpy as jnp
from jax import lax
from jax.experimental import pallas as pl
from jax.experimental.pallas import tpu as pltpu
from jax.sharding import PartitionSpec as P

ITERS = 5
RANK = 64
LANES = 128
PIECES = 4
CHUNKS = 8
HIGHEST = lax.Precision.HIGHEST


def dot_f32(a, b, dims=((1,), (0,))):
    return lax.dot_general(
        a, b, (dims, ((), ())), precision=HIGHEST, preferred_element_type=jnp.float32
    )


def tree_sum(parts):
    parts = list(parts)
    while len(parts) > 1:
        merged = [parts[i] + parts[i + 1] for i in range(0, len(parts) - 1, 2)]
        if len(parts) % 2:
            merged.append(parts[-1])
        parts = merged
    return parts[0]


def swap_halves(x):
    return pltpu.roll(x, RANK, 1)


def lane_of(shape):
    return lax.broadcasted_iota(jnp.int32, shape, 1)


def row_of(shape):
    return lax.broadcasted_iota(jnp.int32, shape, 0)


def inverse_of(tiles):
    tiles = list(tiles)
    shape = (8, LANES)
    row = row_of(shape)
    for b in range(8):
        first = 8 * b
        top = tiles[b]
        spread = [jnp.broadcast_to(top[:, first + c : first + c + 1], shape) for c in range(8)]
        for k in range(8):
            scale = 1.0 / jnp.broadcast_to(spread[k][k : k + 1], shape)
            pivot = jnp.broadcast_to(top[k : k + 1], shape) * scale
            top = jnp.where(row == k, pivot, top - spread[k] * pivot)
            for c in range(k + 1, 8):
                entry = jnp.broadcast_to(spread[c][k : k + 1], shape) * scale
                spread[c] = jnp.where(row == k, entry, spread[c] - spread[k] * entry)
        pivots = [jnp.broadcast_to(top[c : c + 1], shape) for c in range(8)]
        for t in range(8):
            if t == b:
                continue
            terms = [
                jnp.broadcast_to(tiles[t][:, first + c : first + c + 1], shape) * pivots[c]
                for c in range(8)
            ]
            tiles[t] = tiles[t] - tree_sum(terms)
        tiles[b] = top
    return jnp.concatenate(tiles, axis=0)


def both_sides(right):
    left = lane_of(right.shape) < RANK
    return jnp.concatenate(
        [jnp.where(left, swap_halves(right), 0.0), jnp.where(left, 0.0, right)], axis=0
    )


class Ring:
    def __init__(self, axis, n, offset, send, recv, total, sems):
        self.axis, self.n = axis, n
        self.stride = {32: 9, 16: 5}.get(n, n // PIECES)
        self.offset = offset
        self.me = lax.axis_index(axis)
        self.send, self.recv, self.total, self.sems = send, recv, total, sems
        self.owns = lax.rem(self.me, self.stride) == offset
        self.piece = lax.div(self.me, self.stride)

    def copy(self, src, dst, peer, phase):
        return pltpu.make_async_remote_copy(
            src_ref=src,
            dst_ref=dst,
            send_sem=self.sems.at[2 * phase],
            recv_sem=self.sems.at[2 * phase + 1],
            device_id={self.axis: peer},
            device_id_type=pl.DeviceIdType.MESH,
        )

    def scatter(self):
        n = self.n
        for p in range(PIECES):
            owner = self.stride * p + self.offset
            slot = lax.rem(self.me - owner + n, n) - 1

            @pl.when(self.me != owner)
            def _():
                self.copy(self.send.at[p], self.recv.at[slot], owner, 0).start()

    def gather(self):
        n = self.n

        @pl.when(self.owns)
        def _():
            self.copy(self.recv, self.recv, 0, 0).wait_recv()
            self.total[self.piece] = tree_sum(
                [self.send[self.piece]] + [self.recv[k] for k in range(n - 1)]
            )

            @pl.loop(1, n)
            def _(k):
                peer = lax.rem(self.me + k, n)
                self.copy(
                    self.total.at[self.piece], self.total.at[self.piece], peer, 1
                ).start()

    def finish(self):
        @pl.when(self.owns)
        def _():
            some = self.total.at[pl.ds(0, PIECES - 1)]
            self.copy(some, some, 0, 1).wait_recv()
            self.copy(some, some, 0, 0).wait_send()
            self.copy(self.recv, self.recv, 0, 1).wait_send()

        @pl.when(jnp.logical_not(self.owns))
        def _():
            self.copy(self.total, self.total, 0, 1).wait_recv()
            self.copy(self.total, self.total, 0, 0).wait_send()

        return self.total[...].reshape(8 * PIECES, LANES)


def kernel(
    n_cmp,
    n_tgt,
    x_hbm,
    init_ref,
    cond_ref,
    compound_out,
    target_out,
    x_ref,
    inner,
    cond_gram,
    raw_ref,
    side_ref,
    tg_send,
    tg_recv,
    tg_total,
    cg_send,
    cg_recv,
    cg_total,
    cs_send,
    cs_recv,
    cs_total,
    f_send,
    f_recv,
    f_total,
    d_send,
    d_recv,
    x_sems,
    tg_sems,
    cg_sems,
    cs_sems,
    f_sems,
    d_sems,
):
    me_c = lax.axis_index("cmp")
    me_t = lax.axis_index("tgt")
    half = inner.shape[0]
    per = half // CHUNKS
    rows = half // n_tgt

    def fetch(c):
        return [
            pltpu.make_async_copy(
                x_hbm.at[pl.ds(h * half + c * per, per)],
                x_ref.at[pl.ds(h * half + c * per, per)],
                x_sems.at[2 * c + h],
            )
            for h in range(2)
        ]

    for c in range(CHUNKS):
        for one in fetch(c):
            one.start()

    barrier = pltpu.get_barrier_semaphore()

    @pl.loop(1, n_cmp)
    def _(k):
        pl.semaphore_signal(
            barrier,
            inc=1,
            device_id={"cmp": lax.rem(me_c + k, n_cmp)},
            device_id_type=pl.DeviceIdType.MESH,
        )

    @pl.loop(1, n_tgt)
    def _(k):
        pl.semaphore_signal(
            barrier,
            inc=1,
            device_id={"tgt": lax.rem(me_t + k, n_tgt)},
            device_id_type=pl.DeviceIdType.MESH,
        )

    full = (RANK, LANES)
    packed = (8 * PIECES, LANES)
    left_full = lane_of(full) < RANK
    left = lane_of(packed) < RANK
    eye = (lane_of(full) == row_of(full) + RANK).astype(jnp.float32)
    pair = jnp.logical_or(lane_of(full) == row_of(full), lane_of(full) == row_of(full) + RANK)
    twice = pair.astype(jnp.bfloat16)

    cond = cond_ref[...]
    cond_twice = lax.dot_general(
        cond, twice, (((0,), (0,)), ((), ())), preferred_element_type=jnp.float32
    )
    cond_gram[...] = lax.dot_general(
        cond_twice.astype(jnp.bfloat16),
        cond_twice.astype(jnp.bfloat16),
        (((0,), (0,)), ((), ())),
        preferred_element_type=jnp.float32,
    )[:RANK]
    wide_left = lane_of(cond_twice.shape) < RANK
    weights = jnp.concatenate(
        [jnp.where(wide_left, cond_twice, 0.0), jnp.where(wide_left, 0.0, cond_twice)], axis=0
    ).astype(jnp.bfloat16)

    for c in range(CHUNKS):
        for one in fetch(c):
            one.wait()

        @pl.loop(0, per // 8)
        def _(s):
            at = c * per + s * 8
            block = jnp.concatenate([x_ref[pl.ds(at, 8)], x_ref[pl.ds(half + at, 8)]], axis=2)
            flat = block.reshape(8 * RANK, 2 * LANES)
            made = jnp.dot(flat, weights, preferred_element_type=jnp.float32)
            inner[pl.ds(at, 8)] = made.reshape(8, RANK, LANES)

    tg = Ring("tgt", n_tgt, 0, tg_send, tg_recv, tg_total, tg_sems)
    cg = Ring("cmp", n_cmp, 0, cg_send, cg_recv, cg_total, cg_sems)
    cs_offset = {32: 4}.get(n_cmp, 1)
    cs = Ring("cmp", n_cmp, cs_offset, cs_send, cs_recv, cs_total, cs_sems)

    def f_copy(src, dst, peer, phase):
        return pltpu.make_async_remote_copy(
            src_ref=src,
            dst_ref=dst,
            send_sem=f_sems.at[2 * phase],
            recv_sem=f_sems.at[2 * phase + 1],
            device_id={"tgt": peer},
            device_id_type=pl.DeviceIdType.MESH,
        )

    def normal_inverse(total):
        whole = jnp.concatenate([total, swap_halves(total)], axis=0)
        whole = jnp.where(left_full, whole * cond_gram[...], eye)
        return both_sides(inverse_of([whole[8 * t : 8 * t + 8] for t in range(8)]))

    side_ref[...] = jnp.dot(init_ref[...], twice, preferred_element_type=jnp.float32)
    pl.semaphore_wait(barrier, n_cmp + n_tgt - 2)

    @pl.loop(0, ITERS)
    def _(sweep):
        target = side_ref[...]
        square = dot_f32(target, target, ((0,), (0,)))
        tg_send[...] = jnp.where(left, square[:32], square[32:64]).reshape(tg_send.shape)
        tg.scatter()

        def block_of(owner):
            sums = []
            for s in range(0, rows, 8):
                part = inner[pl.ds(owner * rows + s, 8)]
                sums.append(jnp.sum(part * target[None], axis=1))
            return jnp.concatenate(sums, axis=0) if len(sums) > 1 else sums[0]

        @pl.loop(1, n_tgt)
        def _(k):
            peer = lax.rem(me_t + k, n_tgt)
            f_send[peer] = block_of(peer)
            f_copy(f_send.at[peer], f_recv.at[k - 1], peer, 0).start()

        mine = block_of(me_t)
        tg.gather()
        f_copy(f_recv, f_recv, 0, 0).wait_recv()
        f_total[me_t] = tree_sum([mine] + [f_recv[k] for k in range(n_tgt - 1)])

        @pl.loop(1, n_tgt)
        def _(k):
            peer = lax.rem(me_t + k, n_tgt)
            f_copy(f_total.at[me_t], f_total.at[me_t], peer, 1).start()

        across = normal_inverse(tg.finish())
        f_copy(f_recv, f_recv, 0, 0).wait_send()
        f_copy(f_recv, f_recv, 0, 1).wait()
        compound = dot_f32(f_total[...].reshape(half, LANES), across)
        raw_ref[...] = compound

        square = dot_f32(compound, compound, ((0,), (0,)))
        low = square[:32] + swap_halves(square[64:96])
        high = swap_halves(square[32:64]) + square[96:128]
        cg_send[...] = jnp.where(left, low, high).reshape(cg_send.shape)
        cg.scatter()

        def add_rows(s, sums):
            sums = list(sums)
            for d in range(8):
                at = s * 8 + d
                line = jnp.broadcast_to(raw_ref[pl.ds(at, 1), :], (8, LANES))
                for t in range(8):
                    sums[t] = sums[t] + inner[at, 8 * t : 8 * t + 8, :] * line
            return tuple(sums)

        zero = jnp.zeros((8, LANES), jnp.float32)
        sums = lax.fori_loop(0, half // 8, add_rows, (zero,) * 8)
        for p in range(PIECES):
            top = sums[p] + swap_halves(sums[p])
            bottom = sums[p + 4] + swap_halves(sums[p + 4])
            cs_send[p] = jnp.where(left[:8], top, bottom)
        cs.scatter()
        cg.gather()
        cs.gather()
        across = normal_inverse(cg.finish())
        both = dot_f32(cs.finish(), across)
        other = swap_halves(both)
        side_ref[...] = jnp.concatenate(
            [jnp.where(left, both, other), jnp.where(left, other, both)], axis=0
        )

    target = side_ref[...]
    d_send[...] = tree_sum([target[8 * t : 8 * t + 8] * target[8 * t : 8 * t + 8] for t in range(8)])

    def d_copy(src, dst, peer):
        return pltpu.make_async_remote_copy(
            src_ref=src,
            dst_ref=dst,
            send_sem=d_sems.at[0],
            recv_sem=d_sems.at[1],
            device_id={"tgt": peer},
            device_id_type=pl.DeviceIdType.MESH,
        )

    @pl.loop(1, n_tgt)
    def _(k):
        d_copy(d_send, d_recv.at[k - 1], lax.rem(me_t + k, n_tgt)).start()

    total = cg_total[...].reshape(packed)
    other = swap_halves(total)
    whole = jnp.concatenate([jnp.where(left, total, other), jnp.where(left, other, total)], axis=0)
    diagonal = jnp.sum(jnp.where(pair, whole, 0.0), axis=0, keepdims=True)
    compound_count = 2 * half * n_cmp
    scaled = (raw_ref[...] / jnp.sqrt(diagonal / compound_count + 1e-06)).T
    compound_out[:, :half] = scaled[:RANK]
    compound_out[:, half:] = scaled[RANK:]

    d_copy(d_recv, d_recv, 0).wait()
    squares = tree_sum([d_send[...]] + [d_recv[k] for k in range(n_tgt - 1)])
    diagonal = jnp.sum(squares, axis=0, keepdims=True)
    target_count = RANK * n_tgt
    scaled = target / jnp.sqrt(diagonal / target_count + 1e-06)
    target_out[...] = scaled[:, :RANK]


def body(n_cmp, n_tgt, responses, target_init, condition_factor):
    cmp_rows, tgt_rows, cond_count = responses.shape
    half = cmp_rows // 2
    rows = half // n_tgt
    vmem = pltpu.VMEM
    f32 = jnp.float32

    def ring(n):
        return [vmem((PIECES, 8, LANES), f32), vmem((n - 1, 8, LANES), f32), vmem((PIECES, 8, LANES), f32)]

    compound, target = pl.pallas_call(
        functools.partial(kernel, n_cmp, n_tgt),
        out_shape=(
            jax.ShapeDtypeStruct((RANK, cmp_rows), f32),
            jax.ShapeDtypeStruct((tgt_rows, RANK), f32),
        ),
        in_specs=[
            pl.BlockSpec(memory_space=pl.ANY),
            pl.BlockSpec(memory_space=vmem),
            pl.BlockSpec(memory_space=vmem),
        ],
        out_specs=(pl.BlockSpec(memory_space=vmem), pl.BlockSpec(memory_space=vmem)),
        scratch_shapes=[
            vmem((cmp_rows, tgt_rows, cond_count), jnp.bfloat16),
            vmem((half, tgt_rows, LANES), f32),
            vmem((RANK, LANES), f32),
            vmem((half, LANES), f32),
            vmem((tgt_rows, LANES), f32),
            *ring(n_tgt),
            *ring(n_cmp),
            *ring(n_cmp),
            vmem((n_tgt, rows, LANES), f32),
            vmem((n_tgt - 1, rows, LANES), f32),
            vmem((n_tgt, rows, LANES), f32),
            vmem((8, LANES), f32),
            vmem((n_tgt - 1, 8, LANES), f32),
            pltpu.SemaphoreType.DMA((2 * CHUNKS,)),
            pltpu.SemaphoreType.DMA((4,)),
            pltpu.SemaphoreType.DMA((4,)),
            pltpu.SemaphoreType.DMA((4,)),
            pltpu.SemaphoreType.DMA((4,)),
            pltpu.SemaphoreType.DMA((2,)),
        ],
        compiler_params=pltpu.CompilerParams(
            collective_id=0, has_side_effects=True, vmem_limit_bytes=48 * 1024 * 1024
        ),
        cost_estimate=pl.CostEstimate(
            flops=2 * cmp_rows * tgt_rows * RANK * (cond_count + 2 * ITERS),
            bytes_accessed=2 * cmp_rows * tgt_rows * cond_count,
            transcendentals=0,
        ),
    )(responses, target_init, condition_factor.T)
    return compound.T, target


def solution(mesh):
    return jax.shard_map(
        functools.partial(body, mesh.shape["cmp"], mesh.shape["tgt"]),
        mesh=mesh,
        in_specs=(P("cmp", "tgt", None), P("tgt", None), P()),
        out_specs=(P("cmp", None), P("tgt", None)),
        check_vma=False,
    )
```

```python
import functools

import jax
import jax.numpy as jnp
from jax import lax
from jax.experimental import pallas as pl
from jax.experimental.pallas import tpu as pltpu
from jax.sharding import PartitionSpec as P

ITERS = 5
RANK = 64
LANES = 128
PIECES = 4
CHUNKS = 8
HIGHEST = lax.Precision.HIGHEST


def dot_f32(a, b, dims=((1,), (0,))):
    return lax.dot_general(
        a, b, (dims, ((), ())), precision=HIGHEST, preferred_element_type=jnp.float32
    )


def tree_sum(parts):
    parts = list(parts)
    while len(parts) > 1:
        merged = [parts[i] + parts[i + 1] for i in range(0, len(parts) - 1, 2)]
        if len(parts) % 2:
            merged.append(parts[-1])
        parts = merged
    return parts[0]


def swap_halves(x):
    return pltpu.roll(x, RANK, 1)


def lane_of(shape):
    return lax.broadcasted_iota(jnp.int32, shape, 1)


def row_of(shape):
    return lax.broadcasted_iota(jnp.int32, shape, 0)


def inverse_of(tiles):
    tiles = list(tiles)
    shape = (8, LANES)
    row = row_of(shape)
    for b in range(8):
        first = 8 * b
        top = tiles[b]
        spread = [jnp.broadcast_to(top[:, first + c : first + c + 1], shape) for c in range(8)]
        for k in range(8):
            scale = 1.0 / jnp.broadcast_to(spread[k][k : k + 1], shape)
            pivot = jnp.broadcast_to(top[k : k + 1], shape) * scale
            top = jnp.where(row == k, pivot, top - spread[k] * pivot)
            for c in range(k + 1, 8):
                entry = jnp.broadcast_to(spread[c][k : k + 1], shape) * scale
                spread[c] = jnp.where(row == k, entry, spread[c] - spread[k] * entry)
        pivots = [jnp.broadcast_to(top[c : c + 1], shape) for c in range(8)]
        for t in range(8):
            if t == b:
                continue
            terms = [
                jnp.broadcast_to(tiles[t][:, first + c : first + c + 1], shape) * pivots[c]
                for c in range(8)
            ]
            tiles[t] = tiles[t] - tree_sum(terms)
        tiles[b] = top
    return jnp.concatenate(tiles, axis=0)


def both_sides(right):
    left = lane_of(right.shape) < RANK
    return jnp.concatenate(
        [jnp.where(left, swap_halves(right), 0.0), jnp.where(left, 0.0, right)], axis=0
    )


def ring_offsets(outer, inner):
    pairs = [(a, b) for a in range(outer) for b in range(inner) if a or b]
    return sorted(pairs, key=lambda p: -(min(p[0], outer - p[0]) + min(p[1], inner - p[1])))


def peer_at(me, offset, outer, inner):
    a = lax.rem(lax.div(me, inner) + offset[0], outer)
    b = lax.rem(lax.rem(me, inner) + offset[1], inner)
    return a * inner + b


def kernel(
    n_cmp,
    n_tgt,
    x_hbm,
    init_hbm,
    cond_hbm,
    compound_out,
    target_out,
    x_ref,
    init_ref,
    cond_ref,
    inner,
    cond_gram,
    raw_ref,
    side_ref,
    tg_part,
    tg_core,
    tg_line,
    tg_total,
    cg_part,
    cg_plane,
    cg_total,
    cs_send,
    cs_recv,
    cs_plane,
    f_send,
    f_recv,
    f_total,
    d_send,
    d_recv,
    x_sems,
    send_sems,
    recv_sems,
    line_sems,
    cg_sems,
    cs_sems,
):
    me_c = lax.axis_index("cmp")
    me_t = lax.axis_index("tgt")
    n_x, n_z = PIECES, n_cmp // PIECES
    n_y = n_tgt // 2
    me_x = lax.rem(me_c, n_x)
    me_y, core = lax.div(me_t, 2), lax.rem(me_t, 2)
    mate = 2 * me_y + 1 - core
    half = inner.shape[0]
    per = half // CHUNKS
    rows = half // n_tgt
    plane = ring_offsets(n_z, n_x)
    line = ring_offsets(n_y, 2)

    def fetch(c):
        return [
            pltpu.make_async_copy(
                x_hbm.at[pl.ds(h * half + c * per, per)],
                x_ref.at[pl.ds(h * half + c * per, per)],
                x_sems.at[2 * c + h],
            )
            for h in range(2)
        ]

    small = [
        pltpu.make_async_copy(cond_hbm, cond_ref, x_sems.at[2 * CHUNKS]),
        pltpu.make_async_copy(init_hbm, init_ref, x_sems.at[2 * CHUNKS + 1]),
    ]
    for one in small:
        one.start()
    for c in range(CHUNKS):
        for one in fetch(c):
            one.start()

    barrier = pltpu.get_barrier_semaphore()
    for offset in plane:
        pl.semaphore_signal(
            barrier,
            inc=1,
            device_id={"cmp": peer_at(me_c, offset, n_z, n_x)},
            device_id_type=pl.DeviceIdType.MESH,
        )
    for offset in line:
        pl.semaphore_signal(
            barrier,
            inc=1,
            device_id={"tgt": peer_at(me_t, offset, n_y, 2)},
            device_id_type=pl.DeviceIdType.MESH,
        )

    def remote(src, dst, send_sem, recv_sem, axis, peer):
        return pltpu.make_async_remote_copy(
            src_ref=src,
            dst_ref=dst,
            send_sem=send_sems.at[send_sem],
            recv_sem=recv_sem,
            device_id={axis: peer},
            device_id_type=pl.DeviceIdType.MESH,
        )

    full = (RANK, LANES)
    packed = (8 * PIECES, LANES)
    left_full = lane_of(full) < RANK
    left = lane_of(packed) < RANK
    eye = (lane_of(full) == row_of(full) + RANK).astype(jnp.float32)
    pair = jnp.logical_or(lane_of(full) == row_of(full), lane_of(full) == row_of(full) + RANK)
    twice = pair.astype(jnp.bfloat16)

    for one in small:
        one.wait()
    cond = cond_ref[...]
    cond_twice = lax.dot_general(
        cond, twice, (((0,), (0,)), ((), ())), preferred_element_type=jnp.float32
    )
    cond_gram[...] = lax.dot_general(
        cond_twice.astype(jnp.bfloat16),
        cond_twice.astype(jnp.bfloat16),
        (((0,), (0,)), ((), ())),
        preferred_element_type=jnp.float32,
    )[:RANK]
    wide_left = lane_of(cond_twice.shape) < RANK
    weights = jnp.concatenate(
        [jnp.where(wide_left, cond_twice, 0.0), jnp.where(wide_left, 0.0, cond_twice)], axis=0
    ).astype(jnp.bfloat16)
    side_ref[...] = jnp.dot(init_ref[...], twice, preferred_element_type=jnp.float32)

    for c in range(CHUNKS):
        for one in fetch(c):
            one.wait()

        @pl.loop(0, per // 8)
        def _(s):
            at = c * per + s * 8
            block = jnp.concatenate([x_ref[pl.ds(at, 8)], x_ref[pl.ds(half + at, 8)]], axis=2)
            flat = block.reshape(8 * RANK, 2 * LANES)
            made = jnp.dot(flat, weights, preferred_element_type=jnp.float32)
            inner[pl.ds(at, 8)] = made.reshape(8, RANK, LANES)

    def normal_inverse(total):
        whole = jnp.concatenate([total, swap_halves(total)], axis=0)
        whole = jnp.where(left_full, whole * cond_gram[...], eye)
        return both_sides(inverse_of([whole[8 * t : 8 * t + 8] for t in range(8)]))

    def swap_cores(total, index):
        copy = remote(total.at[core], total.at[core], index, recv_sems.at[index], "tgt", mate)
        copy.start()
        return copy

    pl.semaphore_wait(barrier, n_cmp + n_tgt - 2)

    @pl.loop(0, ITERS)
    def _(sweep):
        turn = lax.rem(sweep, 2)

        target = side_ref[...]

        def block_of(owner):
            sums = []
            for s in range(0, rows, 8):
                part = inner[pl.ds(owner * rows + s, 8)]
                sums.append(jnp.sum(part * target[None], axis=1))
            return jnp.concatenate(sums, axis=0) if len(sums) > 1 else sums[0]

        def f_copy(src, dst, phase, peer):
            return remote(src, dst, phase, recv_sems.at[phase], "tgt", peer)

        for offset in line:
            peer = peer_at(me_t, offset, n_y, 2)
            slot = lax.rem(me_t - peer + n_tgt, n_tgt) - 1
            f_send[peer] = block_of(peer)
            f_copy(f_send.at[peer], f_recv.at[slot], 0, peer).start()

        square = dot_f32(target, target, ((0,), (0,)))
        tg_part[...] = jnp.where(left, square[:32], square[32:64]).reshape(tg_part.shape)
        to_mate = remote(tg_part.at[1 - core], tg_core, 2, recv_sems.at[2], "tgt", mate)
        to_mate.start()
        mine = block_of(me_t)
        to_mate.wait_recv()
        tg_line[turn, me_y] = tg_part[core] + tg_core[...]
        own = tg_line.at[turn, me_y]
        for offset in line:
            if offset[1] == 0:
                peer = peer_at(me_t, offset, n_y, 2)
                remote(own, own, 3, line_sems.at[turn], "tgt", peer).start()

        f_copy(f_recv, f_recv, 0, mate).wait_recv()
        f_total[me_t] = tree_sum([mine] + [f_recv[k] for k in range(n_tgt - 1)])
        for offset in line:
            peer = peer_at(me_t, offset, n_y, 2)
            f_copy(f_total.at[me_t], f_total.at[me_t], 1, peer).start()

        others = tg_line.at[turn, pl.ds(0, n_y - 1)]
        remote(others, others, 3, line_sems.at[turn], "tgt", mate).wait_recv()
        tg_total[core] = tree_sum([tg_line[turn, k] for k in range(n_y)])
        swap = swap_cores(tg_total, 4)
        swap.wait_recv()
        across = normal_inverse(tg_total[...].reshape(packed))
        f_copy(f_recv, f_recv, 1, mate).wait_recv()
        compound = dot_f32(f_total[...].reshape(half, LANES), across)
        raw_ref[...] = compound

        def add_rows(s, sums):
            sums = list(sums)
            for d in range(8):
                at = s * 8 + d
                spread = jnp.broadcast_to(raw_ref[pl.ds(at, 1), :], (8, LANES))
                for t in range(8):
                    sums[t] = sums[t] + inner[at, 8 * t : 8 * t + 8, :] * spread
            return tuple(sums)

        zero = jnp.zeros((8, LANES), jnp.float32)
        sums = lax.fori_loop(0, half // 8, add_rows, (zero,) * 8)
        for p in range(PIECES):
            top = sums[p] + swap_halves(sums[p])
            bottom = sums[p + 4] + swap_halves(sums[p + 4])
            cs_send[p] = jnp.where(left[:8], top, bottom)
        for d in (2, 1, 3):
            x = lax.rem(me_x + d, n_x)
            peer = me_c - me_x + x
            remote(cs_send.at[x], cs_recv.at[d - 1], 5, recv_sems.at[5], "cmp", peer).start()

        square = dot_f32(compound, compound, ((0,), (0,)))
        low = square[:32] + swap_halves(square[64:96])
        high = swap_halves(square[32:64]) + square[96:128]
        cg_part[...] = jnp.where(left, low, high).reshape(cg_part.shape)
        cg_plane[turn, me_c] = cg_part[core]
        own = cg_plane.at[turn, me_c]
        for offset in plane:
            peer = peer_at(me_c, offset, n_z, n_x)
            remote(own, own, 6, cg_sems.at[turn], "cmp", peer).start()

        remote(cs_recv, cs_recv, 5, recv_sems.at[5], "cmp", me_c).wait_recv()
        cs_plane[turn, me_c] = (cs_send[me_x] + cs_recv[0]) + (cs_recv[1] + cs_recv[2])
        own = cs_plane.at[turn, me_c]
        for offset in plane:
            peer = peer_at(me_c, offset, n_z, n_x)
            remote(own, own, 7, cs_sems.at[turn], "cmp", peer).start()

        others = cg_plane.at[turn, pl.ds(0, n_cmp - 1)]
        cg_all = remote(others, others, 6, cg_sems.at[turn], "cmp", me_c)
        cg_all.wait_recv()
        cg_total[core] = tree_sum([cg_plane[turn, k] for k in range(n_cmp)])
        swap_c = swap_cores(cg_total, 8)
        swap_c.wait_recv()
        across = normal_inverse(cg_total[...].reshape(packed))
        others = cs_plane.at[turn, pl.ds(0, n_cmp - 1)]
        cs_all = remote(others, others, 7, cs_sems.at[turn], "cmp", me_c)
        cs_all.wait_recv()
        pieces = [
            tree_sum([cs_plane[turn, z * n_x + p] for z in range(n_z)]) for p in range(PIECES)
        ]
        both = dot_f32(jnp.concatenate(pieces, axis=0), across)
        other = swap_halves(both)
        side_ref[...] = jnp.concatenate(
            [jnp.where(left, both, other), jnp.where(left, other, both)], axis=0
        )

        f_copy(f_recv, f_recv, 0, mate).wait_send()
        f_copy(f_recv, f_recv, 1, mate).wait_send()
        to_mate.wait_send()
        others = tg_line.at[turn, pl.ds(0, n_y - 1)]
        remote(others, others, 3, line_sems.at[turn], "tgt", mate).wait_send()
        swap.wait_send()
        remote(cs_recv, cs_recv, 5, recv_sems.at[5], "cmp", me_c).wait_send()
        cg_all.wait_send()
        cs_all.wait_send()
        swap_c.wait_send()

    target = side_ref[...]
    d_send[...] = tree_sum([target[8 * t : 8 * t + 8] * target[8 * t : 8 * t + 8] for t in range(8)])
    for offset in line:
        peer = peer_at(me_t, offset, n_y, 2)
        slot = lax.rem(me_t - peer + n_tgt, n_tgt) - 1
        remote(d_send, d_recv.at[slot], 9, recv_sems.at[9], "tgt", peer).start()

    total = cg_total[...].reshape(packed)
    other = swap_halves(total)
    whole = jnp.concatenate([jnp.where(left, total, other), jnp.where(left, other, total)], axis=0)
    diagonal = jnp.sum(jnp.where(pair, whole, 0.0), axis=0, keepdims=True)
    compound_count = 2 * half * n_cmp
    scaled = (raw_ref[...] / jnp.sqrt(diagonal / compound_count + 1e-06)).T
    compound_out[:, :half] = scaled[:RANK]
    compound_out[:, half:] = scaled[RANK:]

    remote(d_recv, d_recv, 9, recv_sems.at[9], "tgt", mate).wait()
    squares = tree_sum([d_send[...]] + [d_recv[k] for k in range(n_tgt - 1)])
    diagonal = jnp.sum(squares, axis=0, keepdims=True)
    target_count = RANK * n_tgt
    scaled = target / jnp.sqrt(diagonal / target_count + 1e-06)
    target_out[...] = scaled[:, :RANK]


def body(n_cmp, n_tgt, responses, target_init, condition_factor):
    cmp_rows, tgt_rows, cond_count = responses.shape
    half = cmp_rows // 2
    rows = half // n_tgt
    vmem = pltpu.VMEM
    f32 = jnp.float32

    compound, target = pl.pallas_call(
        functools.partial(kernel, n_cmp, n_tgt),
        out_shape=(
            jax.ShapeDtypeStruct((RANK, cmp_rows), f32),
            jax.ShapeDtypeStruct((tgt_rows, RANK), f32),
        ),
        in_specs=[pl.BlockSpec(memory_space=pltpu.HBM)] * 3,
        out_specs=(pl.BlockSpec(memory_space=vmem), pl.BlockSpec(memory_space=vmem)),
        scratch_shapes=[
            vmem((cmp_rows, tgt_rows, cond_count), jnp.bfloat16),
            vmem(target_init.shape, jnp.bfloat16),
            vmem((RANK, cond_count), jnp.bfloat16),
            vmem((half, tgt_rows, LANES), f32),
            vmem((RANK, LANES), f32),
            vmem((half, LANES), f32),
            vmem((tgt_rows, LANES), f32),
            vmem((2, 16, LANES), f32),
            vmem((16, LANES), f32),
            vmem((2, n_tgt // 2, 16, LANES), f32),
            vmem((2, 16, LANES), f32),
            vmem((2, 16, LANES), f32),
            vmem((2, n_cmp, 16, LANES), f32),
            vmem((2, 16, LANES), f32),
            vmem((PIECES, 8, LANES), f32),
            vmem((PIECES - 1, 8, LANES), f32),
            vmem((2, n_cmp, 8, LANES), f32),
            vmem((n_tgt, rows, LANES), f32),
            vmem((n_tgt - 1, rows, LANES), f32),
            vmem((n_tgt, rows, LANES), f32),
            vmem((8, LANES), f32),
            vmem((n_tgt - 1, 8, LANES), f32),
            pltpu.SemaphoreType.DMA((2 * CHUNKS + 2,)),
            pltpu.SemaphoreType.DMA((10,)),
            pltpu.SemaphoreType.DMA((10,)),
            pltpu.SemaphoreType.DMA((2,)),
            pltpu.SemaphoreType.DMA((2,)),
            pltpu.SemaphoreType.DMA((2,)),
        ],
        compiler_params=pltpu.CompilerParams(
            collective_id=0, has_side_effects=True, vmem_limit_bytes=62 * 1024 * 1024
        ),
        cost_estimate=pl.CostEstimate(
            flops=2 * cmp_rows * tgt_rows * RANK * (cond_count + 2 * ITERS),
            bytes_accessed=2 * cmp_rows * tgt_rows * cond_count,
            transcendentals=0,
        ),
    )(responses, target_init, condition_factor.T)
    return compound.T, target


def solution(mesh):
    return jax.shard_map(
        functools.partial(body, mesh.shape["cmp"], mesh.shape["tgt"]),
        mesh=mesh,
        in_specs=(P("cmp", "tgt", None), P("tgt", None), P()),
        out_specs=(P("cmp", None), P("tgt", None)),
        check_vma=False,
    )
```

```python
import functools

import jax
import jax.numpy as jnp
from jax import lax
from jax.experimental import pallas as pl
from jax.experimental.pallas import tpu as pltpu
from jax.sharding import PartitionSpec as P

ITERS = 5
RANK = 64
LANES = 128
PIECES = 4
CHUNKS = 8
HIGHEST = lax.Precision.HIGHEST


def dot_f32(a, b, dims=((1,), (0,))):
    return lax.dot_general(
        a, b, (dims, ((), ())), precision=HIGHEST, preferred_element_type=jnp.float32
    )


def tree_sum(parts):
    parts = list(parts)
    while len(parts) > 1:
        merged = [parts[i] + parts[i + 1] for i in range(0, len(parts) - 1, 2)]
        if len(parts) % 2:
            merged.append(parts[-1])
        parts = merged
    return parts[0]


def swap_halves(x):
    return pltpu.roll(x, RANK, 1)


def lane_of(shape):
    return lax.broadcasted_iota(jnp.int32, shape, 1)


def row_of(shape):
    return lax.broadcasted_iota(jnp.int32, shape, 0)


def inverse_of(tiles):
    tiles = list(tiles)
    shape = (8, LANES)
    row = row_of(shape)
    for b in range(8):
        first = 8 * b
        top = tiles[b]
        spread = [jnp.broadcast_to(top[:, first + c : first + c + 1], shape) for c in range(8)]
        for k in range(8):
            scale = 1.0 / jnp.broadcast_to(spread[k][k : k + 1], shape)
            pivot = jnp.broadcast_to(top[k : k + 1], shape) * scale
            top = jnp.where(row == k, pivot, top - spread[k] * pivot)
            for c in range(k + 1, 8):
                entry = jnp.broadcast_to(spread[c][k : k + 1], shape) * scale
                spread[c] = jnp.where(row == k, entry, spread[c] - spread[k] * entry)
        pivots = [jnp.broadcast_to(top[c : c + 1], shape) for c in range(8)]
        for t in range(8):
            if t == b:
                continue
            terms = [
                jnp.broadcast_to(tiles[t][:, first + c : first + c + 1], shape) * pivots[c]
                for c in range(8)
            ]
            tiles[t] = tiles[t] - tree_sum(terms)
        tiles[b] = top
    return jnp.concatenate(tiles, axis=0)


def both_sides(right):
    left = lane_of(right.shape) < RANK
    return jnp.concatenate(
        [jnp.where(left, swap_halves(right), 0.0), jnp.where(left, 0.0, right)], axis=0
    )


def ring_offsets(outer, inner):
    pairs = [(a, b) for a in range(outer) for b in range(inner) if a or b]
    return sorted(pairs, key=lambda p: -(min(p[0], outer - p[0]) + min(p[1], inner - p[1])))


def peer_at(me, offset, outer, inner):
    a = lax.rem(lax.div(me, inner) + offset[0], outer)
    b = lax.rem(lax.rem(me, inner) + offset[1], inner)
    return a * inner + b


def kernel(
    n_cmp,
    n_tgt,
    x_hbm,
    init_hbm,
    cond_hbm,
    compound_out,
    target_out,
    x_ref,
    init_ref,
    cond_ref,
    inner,
    cond_gram,
    raw_ref,
    side_ref,
    tg_part,
    tg_core,
    tg_line,
    tg_total,
    cg_part,
    cg_plane,
    cg_total,
    gram_ref,
    cs_send,
    cs_recv,
    cs_plane,
    f_send,
    f_recv,
    f_total,
    d_send,
    d_recv,
    x_sems,
    send_sems,
    recv_sems,
    line_sems,
    cg_sems,
    cs_sems,
):
    me_c = lax.axis_index("cmp")
    me_t = lax.axis_index("tgt")
    n_x, n_z = PIECES, n_cmp // PIECES
    n_y = n_tgt // 2
    me_x = lax.rem(me_c, n_x)
    me_y, core = lax.div(me_t, 2), lax.rem(me_t, 2)
    mate = 2 * me_y + 1 - core
    half = inner.shape[0]
    per = half // CHUNKS
    rows = half // n_tgt
    plane = ring_offsets(n_z, n_x)
    line = ring_offsets(n_y, 2)

    def fetch(c):
        return [
            pltpu.make_async_copy(
                x_hbm.at[pl.ds(h * half + c * per, per)],
                x_ref.at[pl.ds(h * half + c * per, per)],
                x_sems.at[2 * c + h],
            )
            for h in range(2)
        ]

    small = [
        pltpu.make_async_copy(cond_hbm, cond_ref, x_sems.at[2 * CHUNKS]),
        pltpu.make_async_copy(init_hbm, init_ref, x_sems.at[2 * CHUNKS + 1]),
    ]
    for one in small:
        one.start()
    for c in range(CHUNKS):
        for one in fetch(c):
            one.start()

    barrier = pltpu.get_barrier_semaphore()
    for offset in plane:
        pl.semaphore_signal(
            barrier,
            inc=1,
            device_id={"cmp": peer_at(me_c, offset, n_z, n_x)},
            device_id_type=pl.DeviceIdType.MESH,
        )
    for offset in line:
        pl.semaphore_signal(
            barrier,
            inc=1,
            device_id={"tgt": peer_at(me_t, offset, n_y, 2)},
            device_id_type=pl.DeviceIdType.MESH,
        )

    def remote(src, dst, send_sem, recv_sem, axis, peer):
        return pltpu.make_async_remote_copy(
            src_ref=src,
            dst_ref=dst,
            send_sem=send_sems.at[send_sem],
            recv_sem=recv_sem,
            device_id={axis: peer},
            device_id_type=pl.DeviceIdType.MESH,
        )

    full = (RANK, LANES)
    packed = (8 * PIECES, LANES)
    left_full = lane_of(full) < RANK
    lane, row = lane_of(packed), row_of(packed)
    left = lane < RANK
    eye = (lane_of(full) == row_of(full) + RANK).astype(jnp.float32)
    pair = jnp.logical_or(lane_of(full) == row_of(full), lane_of(full) == row_of(full) + RANK)
    twice = pair.astype(jnp.bfloat16)

    for one in small:
        one.wait()
    cond = cond_ref[...]
    cond_twice = lax.dot_general(
        cond, twice, (((0,), (0,)), ((), ())), preferred_element_type=jnp.float32
    )
    cond_gram[...] = lax.dot_general(
        cond_twice.astype(jnp.bfloat16),
        cond_twice.astype(jnp.bfloat16),
        (((0,), (0,)), ((), ())),
        preferred_element_type=jnp.float32,
    )[:RANK]
    wide_left = lane_of(cond_twice.shape) < RANK
    weights = jnp.concatenate(
        [jnp.where(wide_left, cond_twice, 0.0), jnp.where(wide_left, 0.0, cond_twice)], axis=0
    ).astype(jnp.bfloat16)
    side_ref[...] = jnp.dot(init_ref[...], twice, preferred_element_type=jnp.float32)

    for c in range(CHUNKS):
        for one in fetch(c):
            one.wait()

        @pl.loop(0, per // 8)
        def _(s):
            at = c * per + s * 8
            block = jnp.concatenate([x_ref[pl.ds(at, 8)], x_ref[pl.ds(half + at, 8)]], axis=2)
            flat = block.reshape(8 * RANK, 2 * LANES)
            made = jnp.dot(flat, weights, preferred_element_type=jnp.float32)
            inner[pl.ds(at, 8)] = made.reshape(8, RANK, LANES)

    def normal_inverse(gram):
        whole = jnp.where(left_full, gram * cond_gram[...], eye)
        return both_sides(inverse_of([whole[8 * t : 8 * t + 8] for t in range(8)]))

    def swap_cores(total, index):
        copy = remote(total.at[core], total.at[core], index, recv_sems.at[index], "tgt", mate)
        copy.start()
        return copy

    pl.semaphore_wait(barrier, n_cmp + n_tgt - 2)

    @pl.loop(0, ITERS)
    def _(sweep):
        turn = lax.rem(sweep, 2)

        target = side_ref[...]

        def block_of(owner):
            sums = []
            for s in range(0, rows, 8):
                part = inner[pl.ds(owner * rows + s, 8)]
                sums.append(jnp.sum(part * target[None], axis=1))
            return jnp.concatenate(sums, axis=0) if len(sums) > 1 else sums[0]

        def f_copy(src, dst, phase, peer):
            return remote(src, dst, phase, recv_sems.at[phase], "tgt", peer)

        for offset in line:
            peer = peer_at(me_t, offset, n_y, 2)
            slot = lax.rem(me_t - peer + n_tgt, n_tgt) - 1
            f_send[peer] = block_of(peer)
            f_copy(f_send.at[peer], f_recv.at[slot], 0, peer).start()

        square = dot_f32(target, target, ((0,), (0,)))
        tg_part[...] = jnp.where(left, square[:32], square[32:64]).reshape(tg_part.shape)
        to_mate = remote(tg_part.at[1 - core], tg_core, 2, recv_sems.at[2], "tgt", mate)
        to_mate.start()
        mine = block_of(me_t)
        to_mate.wait_recv()
        tg_line[turn, me_y] = tg_part[core] + tg_core[...]
        own = tg_line.at[turn, me_y]
        for offset in line:
            if offset[1] == 0:
                peer = peer_at(me_t, offset, n_y, 2)
                remote(own, own, 3, line_sems.at[turn], "tgt", peer).start()

        f_copy(f_recv, f_recv, 0, mate).wait_recv()
        f_total[me_t] = tree_sum([mine] + [f_recv[k] for k in range(n_tgt - 1)])
        for offset in line:
            peer = peer_at(me_t, offset, n_y, 2)
            f_copy(f_total.at[me_t], f_total.at[me_t], 1, peer).start()

        others = tg_line.at[turn, pl.ds(0, n_y - 1)]
        remote(others, others, 3, line_sems.at[turn], "tgt", mate).wait_recv()
        tg_total[core] = tree_sum([tg_line[turn, k] for k in range(n_y)])
        swap = swap_cores(tg_total, 4)
        swap.wait_recv()
        total = tg_total[...].reshape(packed)
        across = normal_inverse(jnp.concatenate([total, swap_halves(total)], axis=0))
        f_copy(f_recv, f_recv, 1, mate).wait_recv()
        compound = dot_f32(f_total[...].reshape(half, LANES), across)
        raw_ref[...] = compound

        def add_rows(s, sums):
            sums = list(sums)
            for d in range(8):
                at = s * 8 + d
                spread = jnp.broadcast_to(raw_ref[pl.ds(at, 1), :], (8, LANES))
                for t in range(8):
                    sums[t] = sums[t] + inner[at, 8 * t : 8 * t + 8, :] * spread
            return tuple(sums)

        zero = jnp.zeros((8, LANES), jnp.float32)
        sums = lax.fori_loop(0, half // 8, add_rows, (zero,) * 8)
        for p in range(PIECES):
            top = sums[p] + swap_halves(sums[p])
            bottom = sums[p + 4] + swap_halves(sums[p + 4])
            cs_send[p] = jnp.where(left[:8], top, bottom)
        for d in (2, 1, 3):
            x = lax.rem(me_x + d, n_x)
            peer = me_c - me_x + x
            remote(cs_send.at[x], cs_recv.at[d - 1], 5, recv_sems.at[5], "cmp", peer).start()

        square = dot_f32(compound, compound, ((0,), (0,)))
        upper = square[:32] + swap_halves(square[64:96])
        lower = pltpu.roll(square[32:64], 96, 1) + pltpu.roll(square[96:128], 32, 1)
        triangles = jnp.where(jnp.logical_and(lane < row, lane < 32), lower, upper)
        folded = jnp.where(left[:16], triangles[:16], swap_halves(triangles[16:]))
        tail = jnp.sum(jnp.where(lane == row, lower, 0.0), axis=0, keepdims=True)
        cg_part[0] = folded[:8]
        cg_part[1] = folded[8:]
        cg_plane[turn, me_c, :8] = cg_part[core]
        cg_plane[turn, me_c, 8:9] = tail
        own = cg_plane.at[turn, me_c, pl.ds(0, 9)]
        for offset in plane:
            peer = peer_at(me_c, offset, n_z, n_x)
            remote(own, own, 6, cg_sems.at[turn], "cmp", peer).start()

        remote(cs_recv, cs_recv, 5, recv_sems.at[5], "cmp", me_c).wait_recv()
        cs_plane[turn, me_c] = (cs_send[me_x] + cs_recv[0]) + (cs_recv[1] + cs_recv[2])
        own = cs_plane.at[turn, me_c]
        for offset in plane:
            peer = peer_at(me_c, offset, n_z, n_x)
            remote(own, own, 7, cs_sems.at[turn], "cmp", peer).start()

        others = cg_plane.at[turn, pl.ds(0, n_cmp - 1), pl.ds(0, 9)]
        cg_all = remote(others, others, 6, cg_sems.at[turn], "cmp", me_c)
        cg_all.wait_recv()
        cg_total[core] = tree_sum([cg_plane[turn, k, :8] for k in range(n_cmp)])
        swap_c = swap_cores(cg_total, 8)
        tail = tree_sum([cg_plane[turn, k, 8:9] for k in range(n_cmp)])
        tail = pltpu.roll(jnp.broadcast_to(0.5 * tail, packed), 32, 1)
        swap_c.wait_recv()
        folded = cg_total[...].reshape(16, LANES)
        triangles = jnp.concatenate([folded, swap_halves(folded)], axis=0)
        upper = jnp.where(lane > row, triangles, jnp.where(lane == row, 0.5 * triangles, 0.0))
        upper = jnp.where(left, upper, 0.0)
        lower = jnp.where(lane < row + 32, pltpu.roll(triangles, 32, 1), 0.0)
        lower = jnp.where(lane == row + 32, tail, lower)
        lower = jnp.where(lane < 32, 0.0, lower)
        one_side = jnp.concatenate([upper, lower, jnp.zeros(full, jnp.float32)], axis=0)
        compound_gram = (one_side + one_side.T)[:RANK]
        gram_ref[...] = compound_gram
        across = normal_inverse(compound_gram)
        others = cs_plane.at[turn, pl.ds(0, n_cmp - 1)]
        cs_all = remote(others, others, 7, cs_sems.at[turn], "cmp", me_c)
        cs_all.wait_recv()
        pieces = [
            tree_sum([cs_plane[turn, z * n_x + p] for z in range(n_z)]) for p in range(PIECES)
        ]
        both = dot_f32(jnp.concatenate(pieces, axis=0), across)
        other = swap_halves(both)
        side_ref[...] = jnp.concatenate(
            [jnp.where(left, both, other), jnp.where(left, other, both)], axis=0
        )

        f_copy(f_recv, f_recv, 0, mate).wait_send()
        f_copy(f_recv, f_recv, 1, mate).wait_send()
        to_mate.wait_send()
        others = tg_line.at[turn, pl.ds(0, n_y - 1)]
        remote(others, others, 3, line_sems.at[turn], "tgt", mate).wait_send()
        swap.wait_send()
        remote(cs_recv, cs_recv, 5, recv_sems.at[5], "cmp", me_c).wait_send()
        cg_all.wait_send()
        cs_all.wait_send()
        swap_c.wait_send()

    target = side_ref[...]
    d_send[...] = tree_sum([target[8 * t : 8 * t + 8] * target[8 * t : 8 * t + 8] for t in range(8)])
    for offset in line:
        peer = peer_at(me_t, offset, n_y, 2)
        slot = lax.rem(me_t - peer + n_tgt, n_tgt) - 1
        remote(d_send, d_recv.at[slot], 9, recv_sems.at[9], "tgt", peer).start()

    alone = jnp.where(lane_of(full) == row_of(full), gram_ref[...], 0.0)
    diagonal = jnp.sum(alone + swap_halves(alone), axis=0, keepdims=True)
    compound_count = 2 * half * n_cmp
    scaled = (raw_ref[...] / jnp.sqrt(diagonal / compound_count + 1e-06)).T
    compound_out[:, :half] = scaled[:RANK]
    compound_out[:, half:] = scaled[RANK:]

    remote(d_recv, d_recv, 9, recv_sems.at[9], "tgt", mate).wait()
    squares = tree_sum([d_send[...]] + [d_recv[k] for k in range(n_tgt - 1)])
    diagonal = jnp.sum(squares, axis=0, keepdims=True)
    target_count = RANK * n_tgt
    scaled = target / jnp.sqrt(diagonal / target_count + 1e-06)
    target_out[...] = scaled[:, :RANK]


def body(n_cmp, n_tgt, responses, target_init, condition_factor):
    cmp_rows, tgt_rows, cond_count = responses.shape
    half = cmp_rows // 2
    rows = half // n_tgt
    vmem = pltpu.VMEM
    f32 = jnp.float32

    compound, target = pl.pallas_call(
        functools.partial(kernel, n_cmp, n_tgt),
        out_shape=(
            jax.ShapeDtypeStruct((RANK, cmp_rows), f32),
            jax.ShapeDtypeStruct((tgt_rows, RANK), f32),
        ),
        in_specs=[pl.BlockSpec(memory_space=pltpu.HBM)] * 3,
        out_specs=(pl.BlockSpec(memory_space=vmem), pl.BlockSpec(memory_space=vmem)),
        scratch_shapes=[
            vmem((cmp_rows, tgt_rows, cond_count), jnp.bfloat16),
            vmem(target_init.shape, jnp.bfloat16),
            vmem((RANK, cond_count), jnp.bfloat16),
            vmem((half, tgt_rows, LANES), f32),
            vmem((RANK, LANES), f32),
            vmem((half, LANES), f32),
            vmem((tgt_rows, LANES), f32),
            vmem((2, 16, LANES), f32),
            vmem((16, LANES), f32),
            vmem((2, n_tgt // 2, 16, LANES), f32),
            vmem((2, 16, LANES), f32),
            vmem((2, 8, LANES), f32),
            vmem((2, n_cmp, 16, LANES), f32),
            vmem((2, 8, LANES), f32),
            vmem((RANK, LANES), f32),
            vmem((PIECES, 8, LANES), f32),
            vmem((PIECES - 1, 8, LANES), f32),
            vmem((2, n_cmp, 8, LANES), f32),
            vmem((n_tgt, rows, LANES), f32),
            vmem((n_tgt - 1, rows, LANES), f32),
            vmem((n_tgt, rows, LANES), f32),
            vmem((8, LANES), f32),
            vmem((n_tgt - 1, 8, LANES), f32),
            pltpu.SemaphoreType.DMA((2 * CHUNKS + 2,)),
            pltpu.SemaphoreType.DMA((10,)),
            pltpu.SemaphoreType.DMA((10,)),
            pltpu.SemaphoreType.DMA((2,)),
            pltpu.SemaphoreType.DMA((2,)),
            pltpu.SemaphoreType.DMA((2,)),
        ],
        compiler_params=pltpu.CompilerParams(
            collective_id=0, has_side_effects=True, vmem_limit_bytes=53 * 1024 * 1024
        ),
        cost_estimate=pl.CostEstimate(
            flops=2 * cmp_rows * tgt_rows * RANK * (cond_count + 2 * ITERS),
            bytes_accessed=2 * cmp_rows * tgt_rows * cond_count,
            transcendentals=0,
        ),
    )(responses, target_init, condition_factor.T)
    return compound.T, target


def solution(mesh):
    return jax.shard_map(
        functools.partial(body, mesh.shape["cmp"], mesh.shape["tgt"]),
        mesh=mesh,
        in_specs=(P("cmp", "tgt", None), P("tgt", None), P()),
        out_specs=(P("cmp", None), P("tgt", None)),
        check_vma=False,
    )
```

```python
import functools

import jax
import jax.numpy as jnp
from jax import lax
from jax.experimental import pallas as pl
from jax.experimental.pallas import tpu as pltpu
from jax.sharding import PartitionSpec as P

ITERS = 5
RANK = 64
LANES = 128
PIECES = 4
TAIL = 6
CHUNKS = 8
HIGHEST = lax.Precision.HIGHEST


def dot_f32(a, b, dims=((1,), (0,))):
    return lax.dot_general(
        a, b, (dims, ((), ())), precision=HIGHEST, preferred_element_type=jnp.float32
    )


def tree_sum(parts):
    parts = list(parts)
    while len(parts) > 1:
        merged = [parts[i] + parts[i + 1] for i in range(0, len(parts) - 1, 2)]
        if len(parts) % 2:
            merged.append(parts[-1])
        parts = merged
    return parts[0]


def swap_halves(x):
    return pltpu.roll(x, RANK, 1)


def lane_of(shape):
    return lax.broadcasted_iota(jnp.int32, shape, 1)


def row_of(shape):
    return lax.broadcasted_iota(jnp.int32, shape, 0)


def inverse_of(tiles):
    tiles = list(tiles)
    shape = (8, LANES)
    row = row_of(shape)
    for b in range(8):
        first = 8 * b
        top = tiles[b]
        spread = [jnp.broadcast_to(top[:, first + c : first + c + 1], shape) for c in range(8)]
        for k in range(8):
            scale = 1.0 / jnp.broadcast_to(spread[k][k : k + 1], shape)
            pivot = jnp.broadcast_to(top[k : k + 1], shape) * scale
            top = jnp.where(row == k, pivot, top - spread[k] * pivot)
            for c in range(k + 1, 8):
                entry = jnp.broadcast_to(spread[c][k : k + 1], shape) * scale
                spread[c] = jnp.where(row == k, entry, spread[c] - spread[k] * entry)
        pivots = [jnp.broadcast_to(top[c : c + 1], shape) for c in range(8)]
        for t in range(8):
            if t == b:
                continue
            terms = [
                jnp.broadcast_to(tiles[t][:, first + c : first + c + 1], shape) * pivots[c]
                for c in range(8)
            ]
            tiles[t] = tiles[t] - tree_sum(terms)
        tiles[b] = top
    return jnp.concatenate(tiles, axis=0)


def both_sides(right):
    left = lane_of(right.shape) < RANK
    return jnp.concatenate(
        [jnp.where(left, swap_halves(right), 0.0), jnp.where(left, 0.0, right)], axis=0
    )


def ring_offsets(outer, inner):
    pairs = [(a, b) for a in range(outer) for b in range(inner) if a or b]
    return sorted(pairs, key=lambda p: -(min(p[0], outer - p[0]) + min(p[1], inner - p[1])))


def peer_at(me, offset, outer, inner):
    a = lax.rem(lax.div(me, inner) + offset[0], outer)
    b = lax.rem(lax.rem(me, inner) + offset[1], inner)
    return a * inner + b


def kernel(
    n_cmp,
    n_tgt,
    x_hbm,
    small_ref,
    compound_out,
    target_out,
    x_ref,
    inner,
    cond_gram,
    raw_ref,
    side_ref,
    tg_part,
    tg_core,
    tg_line,
    tg_total,
    cg_part,
    cg_plane,
    cg_total,
    gram_ref,
    cs_send,
    cs_recv,
    cs_plane,
    f_send,
    f_recv,
    f_total,
    d_send,
    d_recv,
    x_sems,
    send_sems,
    recv_sems,
    line_sems,
    cg_sems,
    cs_sems,
):
    me_c = lax.axis_index("cmp")
    me_t = lax.axis_index("tgt")
    n_x, n_z = PIECES, n_cmp // PIECES
    n_y = n_tgt // 2
    me_x = lax.rem(me_c, n_x)
    me_y, core = lax.div(me_t, 2), lax.rem(me_t, 2)
    mate = 2 * me_y + 1 - core
    half = inner.shape[0]
    per = half // CHUNKS
    rows = half // n_tgt
    plane = ring_offsets(n_z, n_x)
    line = ring_offsets(n_y, 2)

    def fetch(c):
        return [
            pltpu.make_async_copy(
                x_hbm.at[pl.ds(h * half + c * per, per)],
                x_ref.at[pl.ds(h * half + c * per, per)],
                x_sems.at[2 * c + h],
            )
            for h in range(2)
        ]

    for c in range(CHUNKS):
        for one in fetch(c):
            one.start()

    barrier = pltpu.get_barrier_semaphore()
    for offset in plane:
        pl.semaphore_signal(
            barrier,
            inc=1,
            device_id={"cmp": peer_at(me_c, offset, n_z, n_x)},
            device_id_type=pl.DeviceIdType.MESH,
        )
    for offset in line:
        pl.semaphore_signal(
            barrier,
            inc=1,
            device_id={"tgt": peer_at(me_t, offset, n_y, 2)},
            device_id_type=pl.DeviceIdType.MESH,
        )

    def remote(src, dst, send_sem, recv_sem, axis, peer):
        return pltpu.make_async_remote_copy(
            src_ref=src,
            dst_ref=dst,
            send_sem=send_sems.at[send_sem],
            recv_sem=recv_sem,
            device_id={axis: peer},
            device_id_type=pl.DeviceIdType.MESH,
        )

    full = (RANK, LANES)
    packed = (8 * PIECES, LANES)
    left_full = lane_of(full) < RANK
    lane, row = lane_of(packed), row_of(packed)
    left = lane < RANK
    eye = (lane_of(full) == row_of(full) + RANK).astype(jnp.float32)
    pair = jnp.logical_or(lane_of(full) == row_of(full), lane_of(full) == row_of(full) + RANK)
    twice = pair.astype(jnp.bfloat16)

    cond = small_ref[:, :LANES]
    cond_twice = lax.dot_general(
        cond, twice, (((0,), (0,)), ((), ())), preferred_element_type=jnp.float32
    )
    cond_gram[...] = lax.dot_general(
        cond_twice.astype(jnp.bfloat16),
        cond_twice.astype(jnp.bfloat16),
        (((0,), (0,)), ((), ())),
        preferred_element_type=jnp.float32,
    )[:RANK]
    wide_left = lane_of(cond_twice.shape) < RANK
    weights = jnp.concatenate(
        [jnp.where(wide_left, cond_twice, 0.0), jnp.where(wide_left, 0.0, cond_twice)], axis=0
    ).astype(jnp.bfloat16)
    side_ref[...] = jnp.dot(small_ref[:, LANES:], twice, preferred_element_type=jnp.float32)

    for c in range(CHUNKS):
        for one in fetch(c):
            one.wait()

        @pl.loop(0, per // 8)
        def _(s):
            at = c * per + s * 8
            block = jnp.concatenate([x_ref[pl.ds(at, 8)], x_ref[pl.ds(half + at, 8)]], axis=2)
            flat = block.reshape(8 * RANK, 2 * LANES)
            made = jnp.dot(flat, weights, preferred_element_type=jnp.float32)
            inner[pl.ds(at, 8)] = made.reshape(8, RANK, LANES)

    def normal_inverse(gram):
        whole = jnp.where(left_full, gram * cond_gram[...], eye)
        return both_sides(inverse_of([whole[8 * t : 8 * t + 8] for t in range(8)]))

    def swap_cores(total, index):
        copy = remote(total.at[core], total.at[core], index, recv_sems.at[index], "tgt", mate)
        copy.start()
        return copy

    pl.semaphore_wait(barrier, n_cmp + n_tgt - 2)

    @pl.loop(0, ITERS)
    def _(sweep):
        turn = lax.rem(sweep, 2)

        target = side_ref[...]

        def block_of(owner):
            sums = []
            for s in range(0, rows, 8):
                part = inner[pl.ds(owner * rows + s, 8)]
                sums.append(jnp.sum(part * target[None], axis=1))
            return jnp.concatenate(sums, axis=0) if len(sums) > 1 else sums[0]

        def f_copy(src, dst, phase, peer):
            return remote(src, dst, phase, recv_sems.at[phase], "tgt", peer)

        for offset in line:
            peer = peer_at(me_t, offset, n_y, 2)
            slot = lax.rem(me_t - peer + n_tgt, n_tgt) - 1
            f_send[peer] = block_of(peer)
            f_copy(f_send.at[peer], f_recv.at[slot], 0, peer).start()

        square = dot_f32(target, target, ((0,), (0,)))
        tg_part[...] = jnp.where(left, square[:32], square[32:64]).reshape(tg_part.shape)
        to_mate = remote(tg_part.at[1 - core], tg_core, 2, recv_sems.at[2], "tgt", mate)
        to_mate.start()
        mine = block_of(me_t)
        to_mate.wait_recv()
        tg_line[turn, me_y] = tg_part[core] + tg_core[...]
        own = tg_line.at[turn, me_y]
        for offset in line:
            if offset[1] == 0:
                peer = peer_at(me_t, offset, n_y, 2)
                remote(own, own, 3, line_sems.at[turn], "tgt", peer).start()

        f_copy(f_recv, f_recv, 0, mate).wait_recv()
        f_total[me_t] = tree_sum([mine] + [f_recv[k] for k in range(n_tgt - 1)])
        for offset in line:
            peer = peer_at(me_t, offset, n_y, 2)
            f_copy(f_total.at[me_t], f_total.at[me_t], 1, peer).start()

        others = tg_line.at[turn, pl.ds(0, n_y - 1)]
        remote(others, others, 3, line_sems.at[turn], "tgt", mate).wait_recv()
        tg_total[core] = tree_sum([tg_line[turn, k] for k in range(n_y)])
        swap = swap_cores(tg_total, 4)
        swap.wait_recv()
        total = tg_total[...].reshape(packed)
        across = normal_inverse(jnp.concatenate([total, swap_halves(total)], axis=0))
        f_copy(f_recv, f_recv, 1, mate).wait_recv()
        compound = dot_f32(f_total[...].reshape(half, LANES), across)
        raw_ref[...] = compound

        def add_rows(s, sums):
            for d in range(8):
                at = s * 8 + d
                sums = sums + inner[at] * raw_ref[pl.ds(at, 1), :]
            return sums

        steps = half // 8
        sums = lax.fori_loop(0, steps - TAIL, add_rows, jnp.zeros(full, jnp.float32))
        for step in range(steps - TAIL, steps):
            sums = add_rows(step, sums)
        sums = [sums[8 * t : 8 * t + 8] for t in range(8)]
        square = dot_f32(compound, compound, ((0,), (0,)))
        for p in range(PIECES):
            top = sums[p] + swap_halves(sums[p])
            bottom = sums[p + 4] + swap_halves(sums[p + 4])
            cs_send[p] = jnp.where(left[:8], top, bottom)
        for d in (2, 1, 3):
            x = lax.rem(me_x + d, n_x)
            peer = me_c - me_x + x
            remote(cs_send.at[x], cs_recv.at[d - 1], 5, recv_sems.at[5], "cmp", peer).start()

        upper = square[:32] + swap_halves(square[64:96])
        lower = pltpu.roll(square[32:64], 96, 1) + pltpu.roll(square[96:128], 32, 1)
        triangles = jnp.where(jnp.logical_and(lane < row, lane < 32), lower, upper)
        folded = jnp.where(left[:16], triangles[:16], swap_halves(triangles[16:]))
        tail = jnp.sum(jnp.where(lane == row, lower, 0.0), axis=0, keepdims=True)
        cg_part[0] = folded[:8]
        cg_part[1] = folded[8:]
        cg_plane[turn, me_c, :8] = cg_part[core]
        cg_plane[turn, me_c, 8:9] = tail
        own = cg_plane.at[turn, me_c, pl.ds(0, 9)]
        for offset in plane:
            peer = peer_at(me_c, offset, n_z, n_x)
            remote(own, own, 6, cg_sems.at[turn], "cmp", peer).start()

        remote(cs_recv, cs_recv, 5, recv_sems.at[5], "cmp", me_c).wait_recv()
        cs_plane[turn, me_c] = (cs_send[me_x] + cs_recv[0]) + (cs_recv[1] + cs_recv[2])
        own = cs_plane.at[turn, me_c]
        for offset in plane:
            peer = peer_at(me_c, offset, n_z, n_x)
            remote(own, own, 7, cs_sems.at[turn], "cmp", peer).start()

        others = cg_plane.at[turn, pl.ds(0, n_cmp - 1), pl.ds(0, 9)]
        cg_all = remote(others, others, 6, cg_sems.at[turn], "cmp", me_c)
        cg_all.wait_recv()
        cg_total[core] = tree_sum([cg_plane[turn, k, :8] for k in range(n_cmp)])
        swap_c = swap_cores(cg_total, 8)
        tail = tree_sum([cg_plane[turn, k, 8:9] for k in range(n_cmp)])
        tail = pltpu.roll(jnp.broadcast_to(0.5 * tail, packed), 32, 1)
        swap_c.wait_recv()
        folded = cg_total[...].reshape(16, LANES)
        triangles = jnp.concatenate([folded, swap_halves(folded)], axis=0)
        upper = jnp.where(lane > row, triangles, jnp.where(lane == row, 0.5 * triangles, 0.0))
        upper = jnp.where(left, upper, 0.0)
        lower = jnp.where(lane < row + 32, pltpu.roll(triangles, 32, 1), 0.0)
        lower = jnp.where(lane == row + 32, tail, lower)
        lower = jnp.where(lane < 32, 0.0, lower)
        one_side = jnp.concatenate([upper, lower, jnp.zeros(full, jnp.float32)], axis=0)
        compound_gram = (one_side + one_side.T)[:RANK]
        gram_ref[...] = compound_gram
        across = normal_inverse(compound_gram)
        others = cs_plane.at[turn, pl.ds(0, n_cmp - 1)]
        cs_all = remote(others, others, 7, cs_sems.at[turn], "cmp", me_c)
        cs_all.wait_recv()
        pieces = [
            tree_sum([cs_plane[turn, z * n_x + p] for z in range(n_z)]) for p in range(PIECES)
        ]
        both = dot_f32(jnp.concatenate(pieces, axis=0), across)
        other = swap_halves(both)
        side_ref[...] = jnp.concatenate(
            [jnp.where(left, both, other), jnp.where(left, other, both)], axis=0
        )

        f_copy(f_recv, f_recv, 0, mate).wait_send()
        f_copy(f_recv, f_recv, 1, mate).wait_send()
        to_mate.wait_send()
        others = tg_line.at[turn, pl.ds(0, n_y - 1)]
        remote(others, others, 3, line_sems.at[turn], "tgt", mate).wait_send()
        swap.wait_send()
        remote(cs_recv, cs_recv, 5, recv_sems.at[5], "cmp", me_c).wait_send()
        cg_all.wait_send()
        cs_all.wait_send()
        swap_c.wait_send()

    target = side_ref[...]
    d_send[...] = jnp.sum(target * target, axis=0, keepdims=True)
    for offset in line:
        peer = peer_at(me_t, offset, n_y, 2)
        slot = lax.rem(me_t - peer + n_tgt, n_tgt) - 1
        remote(d_send, d_recv.at[slot], 9, recv_sems.at[9], "tgt", peer).start()

    alone = jnp.where(lane_of(full) == row_of(full), gram_ref[...], 0.0)
    diagonal = jnp.sum(alone + swap_halves(alone), axis=0, keepdims=True)
    compound_count = 2 * half * n_cmp
    scaled = (raw_ref[...] / jnp.sqrt(diagonal / compound_count + 1e-06)).T
    compound_out[:, :half] = scaled[:RANK]
    compound_out[:, half:] = scaled[RANK:]

    remote(d_recv, d_recv, 9, recv_sems.at[9], "tgt", mate).wait()
    diagonal = tree_sum([d_send[...]] + [d_recv[k] for k in range(n_tgt - 1)])
    target_count = RANK * n_tgt
    scaled = target / jnp.sqrt(diagonal / target_count + 1e-06)
    target_out[...] = scaled[:, :RANK]


def body(n_cmp, n_tgt, responses, target_init, condition_factor):
    cmp_rows, tgt_rows, cond_count = responses.shape
    half = cmp_rows // 2
    rows = half // n_tgt
    vmem = pltpu.VMEM
    f32 = jnp.float32

    compound, target = pl.pallas_call(
        functools.partial(kernel, n_cmp, n_tgt),
        out_shape=(
            jax.ShapeDtypeStruct((RANK, cmp_rows), f32),
            jax.ShapeDtypeStruct((tgt_rows, RANK), f32),
        ),
        in_specs=[pl.BlockSpec(memory_space=pltpu.HBM), pl.BlockSpec(memory_space=vmem)],
        out_specs=(pl.BlockSpec(memory_space=vmem), pl.BlockSpec(memory_space=vmem)),
        scratch_shapes=[
            vmem((cmp_rows, tgt_rows, cond_count), jnp.bfloat16),
            vmem((half, tgt_rows, LANES), f32),
            vmem((RANK, LANES), f32),
            vmem((half, LANES), f32),
            vmem((tgt_rows, LANES), f32),
            vmem((2, 16, LANES), f32),
            vmem((16, LANES), f32),
            vmem((2, n_tgt // 2, 16, LANES), f32),
            vmem((2, 16, LANES), f32),
            vmem((2, 8, LANES), f32),
            vmem((2, n_cmp, 16, LANES), f32),
            vmem((2, 8, LANES), f32),
            vmem((RANK, LANES), f32),
            vmem((PIECES, 8, LANES), f32),
            vmem((PIECES - 1, 8, LANES), f32),
            vmem((2, n_cmp, 8, LANES), f32),
            vmem((n_tgt, rows, LANES), f32),
            vmem((n_tgt - 1, rows, LANES), f32),
            vmem((n_tgt, rows, LANES), f32),
            vmem((1, LANES), f32),
            vmem((n_tgt - 1, 1, LANES), f32),
            pltpu.SemaphoreType.DMA((2 * CHUNKS,)),
            pltpu.SemaphoreType.DMA((10,)),
            pltpu.SemaphoreType.DMA((10,)),
            pltpu.SemaphoreType.DMA((2,)),
            pltpu.SemaphoreType.DMA((2,)),
            pltpu.SemaphoreType.DMA((2,)),
        ],
        compiler_params=pltpu.CompilerParams(
            collective_id=0, has_side_effects=True, vmem_limit_bytes=53 * 1024 * 1024
        ),
        cost_estimate=pl.CostEstimate(
            flops=2 * cmp_rows * tgt_rows * RANK * (cond_count + 2 * ITERS),
            bytes_accessed=2 * cmp_rows * tgt_rows * cond_count,
            transcendentals=0,
        ),
    )(responses, jnp.concatenate([condition_factor.T, target_init], axis=1))
    return compound.T, target


def solution(mesh):
    return jax.shard_map(
        functools.partial(body, mesh.shape["cmp"], mesh.shape["tgt"]),
        mesh=mesh,
        in_specs=(P("cmp", "tgt", None), P("tgt", None), P()),
        out_specs=(P("cmp", None), P("tgt", None)),
        check_vma=False,
    )
```

```python
import functools

import jax
import jax.numpy as jnp
from jax import lax
from jax.experimental import pallas as pl
from jax.experimental.pallas import tpu as pltpu
from jax.sharding import PartitionSpec as P

ITERS = 5
RANK = 64
LANES = 128
PIECES = 4
TAIL = 6
CHUNKS = 8
HIGHEST = lax.Precision.HIGHEST


def dot_f32(a, b, dims=((1,), (0,))):
    return lax.dot_general(
        a, b, (dims, ((), ())), precision=HIGHEST, preferred_element_type=jnp.float32
    )


def tree_sum(parts):
    parts = list(parts)
    while len(parts) > 1:
        merged = [parts[i] + parts[i + 1] for i in range(0, len(parts) - 1, 2)]
        if len(parts) % 2:
            merged.append(parts[-1])
        parts = merged
    return parts[0]


def swap_halves(x):
    return pltpu.roll(x, RANK, 1)


def lane_of(shape):
    return lax.broadcasted_iota(jnp.int32, shape, 1)


def row_of(shape):
    return lax.broadcasted_iota(jnp.int32, shape, 0)


def inverse_of(tiles):
    tiles = list(tiles)
    shape = (8, LANES)
    row = row_of(shape)
    for b in range(8):
        first = 8 * b
        top = tiles[b]
        spread = [jnp.broadcast_to(top[:, first + c : first + c + 1], shape) for c in range(8)]
        for k in range(8):
            scale = 1.0 / jnp.broadcast_to(spread[k][k : k + 1], shape)
            pivot = jnp.broadcast_to(top[k : k + 1], shape) * scale
            top = jnp.where(row == k, pivot, top - spread[k] * pivot)
            for c in range(k + 1, 8):
                entry = jnp.broadcast_to(spread[c][k : k + 1], shape) * scale
                spread[c] = jnp.where(row == k, entry, spread[c] - spread[k] * entry)
        pivots = [jnp.broadcast_to(top[c : c + 1], shape) for c in range(8)]
        for t in range(8):
            if t == b:
                continue
            terms = [
                jnp.broadcast_to(tiles[t][:, first + c : first + c + 1], shape) * pivots[c]
                for c in range(8)
            ]
            tiles[t] = tiles[t] - tree_sum(terms)
        tiles[b] = top
    return jnp.concatenate(tiles, axis=0)


def both_sides(right):
    left = lane_of(right.shape) < RANK
    return jnp.concatenate(
        [jnp.where(left, swap_halves(right), 0.0), jnp.where(left, 0.0, right)], axis=0
    )


def ring_offsets(outer, inner):
    pairs = [(a, b) for a in range(outer) for b in range(inner) if a or b]
    return sorted(pairs, key=lambda p: -(min(p[0], outer - p[0]) + min(p[1], inner - p[1])))


def peer_at(me, offset, outer, inner):
    a = lax.rem(lax.div(me, inner) + offset[0], outer)
    b = lax.rem(lax.rem(me, inner) + offset[1], inner)
    return a * inner + b


def kernel(
    n_cmp,
    n_tgt,
    x_hbm,
    small_ref,
    compound_out,
    target_out,
    x_ref,
    inner,
    cond_gram,
    raw_ref,
    side_ref,
    tg_part,
    tg_core,
    tg_line,
    tg_total,
    cg_part,
    cg_plane,
    cg_total,
    gram_ref,
    cs_send,
    cs_recv,
    cs_plane,
    f_send,
    f_recv,
    f_total,
    d_send,
    d_recv,
    x_sems,
    send_sems,
    recv_sems,
    line_sems,
    cg_sems,
    cs_sems,
):
    me_c = lax.axis_index("cmp")
    me_t = lax.axis_index("tgt")
    n_x, n_z = PIECES, n_cmp // PIECES
    n_y = n_tgt // 2
    me_x = lax.rem(me_c, n_x)
    me_y, core = lax.div(me_t, 2), lax.rem(me_t, 2)
    mate = 2 * me_y + 1 - core
    half = inner.shape[0]
    per = half // CHUNKS
    rows = half // n_tgt
    plane = ring_offsets(n_z, n_x)
    line = ring_offsets(n_y, 2)

    def fetch(c):
        return [
            pltpu.make_async_copy(
                x_hbm.at[pl.ds(h * half + c * per, per)],
                x_ref.at[pl.ds(h * half + c * per, per)],
                x_sems.at[2 * c + h],
            )
            for h in range(2)
        ]

    for c in range(CHUNKS):
        for one in fetch(c):
            one.start()

    barrier = pltpu.get_barrier_semaphore()
    for offset in plane:
        pl.semaphore_signal(
            barrier,
            inc=1,
            device_id={"cmp": peer_at(me_c, offset, n_z, n_x)},
            device_id_type=pl.DeviceIdType.MESH,
        )
    for offset in line:
        pl.semaphore_signal(
            barrier,
            inc=1,
            device_id={"tgt": peer_at(me_t, offset, n_y, 2)},
            device_id_type=pl.DeviceIdType.MESH,
        )

    def remote(src, dst, send_sem, recv_sem, axis, peer):
        return pltpu.make_async_remote_copy(
            src_ref=src,
            dst_ref=dst,
            send_sem=send_sems.at[send_sem],
            recv_sem=recv_sem,
            device_id={axis: peer},
            device_id_type=pl.DeviceIdType.MESH,
        )

    full = (RANK, LANES)
    packed = (8 * PIECES, LANES)
    left_full = lane_of(full) < RANK
    lane, row = lane_of(packed), row_of(packed)
    left = lane < RANK
    eye = (lane_of(full) == row_of(full) + RANK).astype(jnp.float32)
    pair = jnp.logical_or(lane_of(full) == row_of(full), lane_of(full) == row_of(full) + RANK)
    twice = pair.astype(jnp.bfloat16)

    cond = small_ref[:, :LANES]
    cond_twice = lax.dot_general(
        cond, twice, (((0,), (0,)), ((), ())), preferred_element_type=jnp.float32
    )
    cond_gram[...] = lax.dot_general(
        cond_twice.astype(jnp.bfloat16),
        cond_twice.astype(jnp.bfloat16),
        (((0,), (0,)), ((), ())),
        preferred_element_type=jnp.float32,
    )[:RANK]
    wide_left = lane_of(cond_twice.shape) < RANK
    weights = jnp.concatenate(
        [jnp.where(wide_left, cond_twice, 0.0), jnp.where(wide_left, 0.0, cond_twice)], axis=0
    ).astype(jnp.bfloat16)
    side_ref[...] = jnp.dot(small_ref[:, LANES:], twice, preferred_element_type=jnp.float32)

    for c in range(CHUNKS):
        for one in fetch(c):
            one.wait()

        @pl.loop(0, per // 8)
        def _(s):
            at = c * per + s * 8
            block = jnp.concatenate([x_ref[pl.ds(at, 8)], x_ref[pl.ds(half + at, 8)]], axis=2)
            flat = block.reshape(8 * RANK, 2 * LANES)
            made = jnp.dot(flat, weights, preferred_element_type=jnp.float32)
            inner[pl.ds(at, 8)] = made.reshape(8, RANK, LANES)

    def normal_inverse(gram):
        whole = jnp.where(left_full, gram * cond_gram[...], eye)
        return both_sides(inverse_of([whole[8 * t : 8 * t + 8] for t in range(8)]))

    def swap_cores(total, index):
        copy = remote(total.at[core], total.at[core], index, recv_sems.at[index], "tgt", mate)
        copy.start()
        return copy

    pl.semaphore_wait(barrier, n_cmp + n_tgt - 2)

    @pl.loop(0, ITERS)
    def _(sweep):
        turn = lax.rem(sweep, 2)

        target = side_ref[...]

        def block_of(owner):
            sums = []
            for s in range(0, rows, 8):
                part = inner[pl.ds(owner * rows + s, 8)]
                sums.append(jnp.sum(part * target[None], axis=1))
            return jnp.concatenate(sums, axis=0) if len(sums) > 1 else sums[0]

        def f_copy(src, dst, phase, peer):
            return remote(src, dst, phase, recv_sems.at[phase], "tgt", peer)

        for offset in line:
            peer = peer_at(me_t, offset, n_y, 2)
            slot = lax.rem(me_t - peer + n_tgt, n_tgt) - 1
            f_send[peer] = block_of(peer)
            f_copy(f_send.at[peer], f_recv.at[slot], 0, peer).start()

        square = dot_f32(target, target, ((0,), (0,)))
        tg_part[...] = jnp.where(left, square[:32], square[32:64]).reshape(tg_part.shape)
        to_mate = remote(tg_part.at[1 - core], tg_core, 2, recv_sems.at[2], "tgt", mate)
        to_mate.start()
        mine = block_of(me_t)
        to_mate.wait_recv()
        tg_line[turn, me_y] = tg_part[core] + tg_core[...]
        own = tg_line.at[turn, me_y]
        for offset in line:
            if offset[1] == 0:
                peer = peer_at(me_t, offset, n_y, 2)
                remote(own, own, 3, line_sems.at[turn], "tgt", peer).start()

        f_copy(f_recv, f_recv, 0, mate).wait_recv()
        f_total[me_t] = tree_sum([mine] + [f_recv[k] for k in range(n_tgt - 1)])
        for offset in line:
            peer = peer_at(me_t, offset, n_y, 2)
            f_copy(f_total.at[me_t], f_total.at[me_t], 1, peer).start()

        others = tg_line.at[turn, pl.ds(0, n_y - 1)]
        remote(others, others, 3, line_sems.at[turn], "tgt", mate).wait_recv()
        tg_total[core] = tree_sum([tg_line[turn, k] for k in range(n_y)])
        swap = swap_cores(tg_total, 4)
        swap.wait_recv()
        total = tg_total[...].reshape(packed)
        across = normal_inverse(jnp.concatenate([total, swap_halves(total)], axis=0))
        f_copy(f_recv, f_recv, 1, mate).wait_recv()
        compound = dot_f32(f_total[...].reshape(half, LANES), across)
        raw_ref[...] = compound

        def add_rows(s, sums):
            for d in range(8):
                at = s * 8 + d
                sums = sums + inner[at] * raw_ref[pl.ds(at, 1), :]
            return sums

        steps = half // 8
        sums = lax.fori_loop(0, steps - TAIL, add_rows, jnp.zeros(full, jnp.float32))
        for step in range(steps - TAIL, steps):
            sums = add_rows(step, sums)
        sums = [sums[8 * t : 8 * t + 8] for t in range(8)]
        square = dot_f32(compound, compound, ((0,), (0,)))
        for p in range(PIECES):
            top = sums[p] + swap_halves(sums[p])
            bottom = sums[p + 4] + swap_halves(sums[p + 4])
            cs_send[p] = jnp.where(left[:8], top, bottom)
        for d in (2, 1, 3):
            x = lax.rem(me_x + d, n_x)
            peer = me_c - me_x + x
            remote(cs_send.at[x], cs_recv.at[d - 1], 5, recv_sems.at[5], "cmp", peer).start()

        upper = square[:32] + swap_halves(square[64:96])
        lower = pltpu.roll(square[32:64], 96, 1) + pltpu.roll(square[96:128], 32, 1)
        triangles = jnp.where(jnp.logical_and(lane < row, lane < 32), lower, upper)
        folded = jnp.where(left[:16], triangles[:16], swap_halves(triangles[16:]))
        tail = jnp.sum(jnp.where(lane == row, lower, 0.0), axis=0, keepdims=True)
        cg_part[0] = folded[:8]
        cg_part[1] = folded[8:]
        cg_plane[turn, me_c, :8] = cg_part[core]
        cg_plane[turn, me_c, 8:9] = tail
        own = cg_plane.at[turn, me_c, pl.ds(0, 9)]
        for offset in plane:
            peer = peer_at(me_c, offset, n_z, n_x)
            remote(own, own, 6, cg_sems.at[turn], "cmp", peer).start()

        remote(cs_recv, cs_recv, 5, recv_sems.at[5], "cmp", me_c).wait_recv()
        cs_plane[turn, me_c] = (cs_send[me_x] + cs_recv[0]) + (cs_recv[1] + cs_recv[2])
        own = cs_plane.at[turn, me_c]
        for offset in plane:
            peer = peer_at(me_c, offset, n_z, n_x)
            remote(own, own, 7, cs_sems.at[turn], "cmp", peer).start()

        others = cg_plane.at[turn, pl.ds(0, n_cmp - 1), pl.ds(0, 9)]
        cg_all = remote(others, others, 6, cg_sems.at[turn], "cmp", me_c)
        cg_all.wait_recv()
        cg_total[core] = tree_sum([cg_plane[turn, k, :8] for k in range(n_cmp)])
        swap_c = swap_cores(cg_total, 8)
        tail = tree_sum([cg_plane[turn, k, 8:9] for k in range(n_cmp)])
        tail = pltpu.roll(jnp.broadcast_to(0.5 * tail, packed), 32, 1)
        swap_c.wait_recv()
        folded = cg_total[...].reshape(16, LANES)
        triangles = jnp.concatenate([folded, swap_halves(folded)], axis=0)
        upper = jnp.where(lane > row, triangles, jnp.where(lane == row, 0.5 * triangles, 0.0))
        upper = jnp.where(left, upper, 0.0)
        lower = jnp.where(lane < row + 32, pltpu.roll(triangles, 32, 1), 0.0)
        lower = jnp.where(lane == row + 32, tail, lower)
        lower = jnp.where(lane < 32, 0.0, lower)
        one_side = jnp.concatenate([upper, lower], axis=0)
        other = one_side.T[:RANK]
        compound_gram = one_side + jnp.concatenate([other, jnp.zeros_like(other)], axis=1)
        gram_ref[...] = compound_gram
        across = normal_inverse(compound_gram)
        others = cs_plane.at[turn, pl.ds(0, n_cmp - 1)]
        cs_all = remote(others, others, 7, cs_sems.at[turn], "cmp", me_c)
        cs_all.wait_recv()
        pieces = [
            tree_sum([cs_plane[turn, z * n_x + p] for z in range(n_z)]) for p in range(PIECES)
        ]
        both = dot_f32(jnp.concatenate(pieces, axis=0), across)
        other = swap_halves(both)
        side_ref[...] = jnp.concatenate(
            [jnp.where(left, both, other), jnp.where(left, other, both)], axis=0
        )

        f_copy(f_recv, f_recv, 0, mate).wait_send()
        f_copy(f_recv, f_recv, 1, mate).wait_send()
        to_mate.wait_send()
        others = tg_line.at[turn, pl.ds(0, n_y - 1)]
        remote(others, others, 3, line_sems.at[turn], "tgt", mate).wait_send()
        swap.wait_send()
        remote(cs_recv, cs_recv, 5, recv_sems.at[5], "cmp", me_c).wait_send()
        cg_all.wait_send()
        cs_all.wait_send()
        swap_c.wait_send()

    target = side_ref[...]
    d_send[...] = jnp.sum(target * target, axis=0, keepdims=True)
    for offset in line:
        peer = peer_at(me_t, offset, n_y, 2)
        slot = lax.rem(me_t - peer + n_tgt, n_tgt) - 1
        remote(d_send, d_recv.at[slot], 9, recv_sems.at[9], "tgt", peer).start()

    alone = jnp.where(lane_of(full) == row_of(full), gram_ref[...], 0.0)
    diagonal = jnp.sum(alone + swap_halves(alone), axis=0, keepdims=True)
    compound_count = 2 * half * n_cmp
    scaled = (raw_ref[...] / jnp.sqrt(diagonal / compound_count + 1e-06)).T
    compound_out[:, :half] = scaled[:RANK]
    compound_out[:, half:] = scaled[RANK:]

    remote(d_recv, d_recv, 9, recv_sems.at[9], "tgt", mate).wait()
    diagonal = tree_sum([d_send[...]] + [d_recv[k] for k in range(n_tgt - 1)])
    target_count = RANK * n_tgt
    scaled = target / jnp.sqrt(diagonal / target_count + 1e-06)
    target_out[...] = scaled[:, :RANK]


def body(n_cmp, n_tgt, responses, target_init, condition_factor):
    cmp_rows, tgt_rows, cond_count = responses.shape
    half = cmp_rows // 2
    rows = half // n_tgt
    vmem = pltpu.VMEM
    f32 = jnp.float32

    compound, target = pl.pallas_call(
        functools.partial(kernel, n_cmp, n_tgt),
        out_shape=(
            jax.ShapeDtypeStruct((RANK, cmp_rows), f32),
            jax.ShapeDtypeStruct((tgt_rows, RANK), f32),
        ),
        in_specs=[pl.BlockSpec(memory_space=pltpu.HBM), pl.BlockSpec(memory_space=vmem)],
        out_specs=(pl.BlockSpec(memory_space=vmem), pl.BlockSpec(memory_space=vmem)),
        scratch_shapes=[
            vmem((cmp_rows, tgt_rows, cond_count), jnp.bfloat16),
            vmem((half, tgt_rows, LANES), f32),
            vmem((RANK, LANES), f32),
            vmem((half, LANES), f32),
            vmem((tgt_rows, LANES), f32),
            vmem((2, 16, LANES), f32),
            vmem((16, LANES), f32),
            vmem((2, n_tgt // 2, 16, LANES), f32),
            vmem((2, 16, LANES), f32),
            vmem((2, 8, LANES), f32),
            vmem((2, n_cmp, 16, LANES), f32),
            vmem((2, 8, LANES), f32),
            vmem((RANK, LANES), f32),
            vmem((PIECES, 8, LANES), f32),
            vmem((PIECES - 1, 8, LANES), f32),
            vmem((2, n_cmp, 8, LANES), f32),
            vmem((n_tgt, rows, LANES), f32),
            vmem((n_tgt - 1, rows, LANES), f32),
            vmem((n_tgt, rows, LANES), f32),
            vmem((1, LANES), f32),
            vmem((n_tgt - 1, 1, LANES), f32),
            pltpu.SemaphoreType.DMA((2 * CHUNKS,)),
            pltpu.SemaphoreType.DMA((10,)),
            pltpu.SemaphoreType.DMA((10,)),
            pltpu.SemaphoreType.DMA((2,)),
            pltpu.SemaphoreType.DMA((2,)),
            pltpu.SemaphoreType.DMA((2,)),
        ],
        compiler_params=pltpu.CompilerParams(
            collective_id=0, has_side_effects=True, vmem_limit_bytes=53 * 1024 * 1024
        ),
        cost_estimate=pl.CostEstimate(
            flops=2 * cmp_rows * tgt_rows * RANK * (cond_count + 2 * ITERS),
            bytes_accessed=2 * cmp_rows * tgt_rows * cond_count,
            transcendentals=0,
        ),
    )(responses, jnp.concatenate([condition_factor.T, target_init], axis=1))
    return compound.T, target


def solution(mesh):
    return jax.shard_map(
        functools.partial(body, mesh.shape["cmp"], mesh.shape["tgt"]),
        mesh=mesh,
        in_specs=(P("cmp", "tgt", None), P("tgt", None), P()),
        out_specs=(P("cmp", None), P("tgt", None)),
        check_vma=False,
    )
```
